512 devices in a mesh: row: 32 (over x_lo, z), col: 16 (over y, x_hi, core).
Axes of the slice: x: 4 (x_hi: 2, x_lo: 2; x = x_hi * 2 + x_lo), y: 4, z: 16, core: 2. Of those that a mesh axis runs over, the one named last changes fastest.
Arguments:
- row_features: bfloat16 [98304, 256], P('row'), may hold values from -6 to 6
- row_vectors: bfloat16 [17, 98304], P(None, 'row'), may hold values from -24 to 24
- slab_features: bfloat16 [3072, 256], P('col', 'row'), may hold values from -6 to 6
- slab_vectors: bfloat16 [17, 3072], P(None, 'col'), may hold values from -24 to 24
Outputs:
- row_grad: float32 [98304, 256], P('row', 'col')
- slab_grad: float32 [3072, 256], P('col', 'row')
The draws below stay inside these ranges and needn't reach their ends.
All inputs are finite; a program needn't handle non-finite values.
Results may differ from the reference program's by a relative error of at most 0.008.
Values may be sent and summed in bfloat16 or wider, within the bound.
A program may use at most 64 MiB of HBM per device.

```python
import jax
import jax.numpy as jnp
from jax import lax

D = 256
SLAB = 3072
PROBES = 16
VECS = 17
NROWS = 98304
N_COL = 16


def block_levels(stream_key, extent, pieces, low, largest):
    loudness, own = 1.0, jax.random.fold_in(stream_key, 6)
    for dim, parts in pieces:
        steps = jnp.exp(jax.random.uniform(jax.random.fold_in(own, dim), (parts,), jnp.float32, low / len(pieces), largest / len(pieces)))
        loudness = loudness * jnp.repeat(steps, extent[dim] // parts).reshape([-1 if axis == dim else 1 for axis in range(len(extent))])
    return loudness


def centred(key, dims, spread, limit, split=(), dtype=jnp.bfloat16):
    entries = jax.random.normal(key, dims, jnp.float32) * spread
    if len(split) > 0:
        entries = block_levels(key, dims, split, -0.22, 0.18) * entries
    return jnp.clip(entries, min=-limit, max=limit).astype(dtype)


def setup_inputs(seed: int = 0) -> dict:
    key_list = jax.random.split(jax.random.key(seed), 5)
    return {
        "row_features": centred(key_list[0], (NROWS, D), 1.0, 6.0, ((0, 32),)),
        "row_vectors": centred(key_list[1], (VECS, NROWS), 4.0, 24.0, ((1, 32),)),
        "slab_features": centred(key_list[2], (SLAB, D), 1.0, 6.0, ((0, 16), (1, 32))),
        "slab_vectors": centred(key_list[3], (VECS, SLAB), 4.0, 24.0, ((1, 16),)),
    }


def weighted(features, vectors, block, block_vectors):
    left_square = jnp.sum(jnp.square(features.astype(jnp.float32)), axis=1)
    right_square = jnp.sum(jnp.square(block.astype(jnp.float32)), axis=1)
    inner = lax.dot_general(features, block, (((1,), (1,)), ((), ())), preferred_element_type=jnp.float32)
    distance = left_square[:, None] + right_square[None, :] - 2.0 * inner
    kernel = jnp.exp(-distance / (2.0 * D))
    factors = jnp.where(jnp.arange(VECS) == 0, 0.5, -0.5 / PROBES)
    scaled = (block_vectors.astype(jnp.float32) * factors[:, None]).astype(jnp.bfloat16)
    coupling = jnp.einsum("kr,kc->rc", vectors, scaled, preferred_element_type=jnp.float32)
    return (coupling * kernel).astype(jnp.bfloat16)


def reference(row_features, row_vectors, slab_features, slab_vectors):
    width = SLAB // N_COL
    blocks = slab_features.reshape(N_COL, width, D)
    block_vecs = slab_vectors.reshape(VECS, N_COL, width).transpose(1, 0, 2)
    rows_wide = row_features.astype(jnp.float32)

    def step(total, pair):
        block, bvec = pair
        weights = weighted(row_features, row_vectors, block, bvec)
        wide = weights.astype(jnp.float32)
        row_term = (jnp.dot(weights, block, preferred_element_type=jnp.float32) - jnp.sum(wide, axis=1)[:, None] * rows_wide) / D
        slab_term = (lax.dot_general(weights, row_features, (((0,), (0,)), ((), ())), preferred_element_type=jnp.float32) - jnp.sum(wide, axis=0)[:, None] * block.astype(jnp.float32)) / D
        return total + row_term, slab_term

    total, slab_terms = lax.scan(step, jnp.zeros((NROWS, D), jnp.float32), (blocks, block_vecs))
    return total, slab_terms.reshape(SLAB, D)
```

```python
import functools

import jax
import jax.numpy as jnp
from jax import lax
from jax.experimental import pallas as pl
from jax.experimental.pallas import tpu as pltpu
from jax.sharding import PartitionSpec as P

D = 256
PROBES = 16
VECS = 17
ROWS = 3072
COLS = 192
N_ROW = 32
CHUNKS = 6
RQ = ROWS // CHUNKS
LAG = (2, 4, 6, 8)
F32, BF16 = jnp.float32, jnp.bfloat16


def kernel(
    sf, sv, rv, rf_hbm,
    row_out, slab_out,
    rf, rft, rsq, coup, slots, slabn, slabp, ssq, acc, wcol,
    kept, s_a, r_a, s_bp, r_bp, s_bm, r_bm, s_cp, r_cp, s_cm, r_cm, s_d, r_d,
    g_own, g_send, g_recv,
    rf_sem, ag_send, ag_recv, g_ssem, g_rsem, st_send, st_recv,
):
    row, col = lax.axis_index("row"), lax.axis_index("col")
    y, hi, core = col // 4, lax.rem(col // 2, 2), lax.rem(col, 2)
    up, down, far = lax.rem(y + 1, 4), lax.rem(y + 3, 4), lax.rem(y + 2, 4)

    def at(y_, hi_, core_):
        return {"row": row, "col": y_ * 4 + hi_ * 2 + core_}

    sibling = at(y, hi, 1 - core)
    above, below, across = at(up, hi, core), at(down, hi, core), at(y, 1 - hi, core)

    load = pltpu.make_async_copy(rf_hbm, rf, rf_sem)
    load.start()

    barrier = pltpu.get_barrier_semaphore()
    for other in (sibling, above, below, across):
        pl.semaphore_signal(barrier, inc=1, device_id=other)

    def greet(d, c):
        pl.semaphore_signal(
            barrier, inc=1, device_id={"row": lax.rem(row + d, N_ROW), "col": col}
        )
        return c

    lax.fori_loop(1, N_ROW, greet, 0)
    pl.semaphore_wait(barrier, N_ROW + 3)

    def gather(peer, slot):
        return pltpu.make_async_remote_copy(
            sf, slots.at[slot], ag_send.at[peer], ag_recv.at[slot],
            device_id={"row": peer, "col": col},
        )

    def send_slab(d, c):
        gather(lax.rem(row + d, N_ROW), row).start()
        return c

    lax.fori_loop(1, N_ROW, send_slab, 0)
    slots[row] = sf[...]

    first = lax.broadcasted_iota(jnp.int32, (VECS, COLS), 0) == 0
    scaled = (sv[...].astype(F32) * jnp.where(first, 0.5, -0.5 / PROBES)).T.astype(BF16)
    load.wait()

    def prepare(q, c):
        wide = rf[pl.ds(pl.multiple_of(q * RQ, RQ), RQ), :].astype(F32).T
        rsq[q] = jnp.sum(wide * wide, axis=0, keepdims=True) * (0.5 / D)
        rft[q] = wide.astype(BF16)
        coup[q] = jnp.dot(
            scaled, rv[:, pl.ds(pl.multiple_of(q * RQ, RQ), RQ)],
            preferred_element_type=F32,
        )
        return c

    lax.fori_loop(0, CHUNKS, prepare, 0)
    acc[...] = jnp.zeros_like(acc)
    wcol[...] = jnp.zeros_like(wcol)

    def got_slab(d, c):
        peer = lax.rem(row + d, N_ROW)
        gather(peer, peer).wait_recv()
        return c

    lax.fori_loop(1, N_ROW, got_slab, 0)

    slab_t = slots[...].astype(F32).reshape(D, COLS)
    slab_n = slab_t.T
    ssq[...] = jnp.broadcast_to(
        jnp.sum(slab_n * slab_n, axis=1, keepdims=True) * (0.5 / D), ssq.shape
    )
    slabn[...] = (slab_n * (1.0 / D)).astype(BF16)
    order = [yy * 4 + hh * 2 + cc for cc in range(2) for yy in range(4) for hh in range(2)]
    slabp[...] = jnp.concatenate(
        [slab_t[g * 16 : g * 16 + 16] * (1.0 / D) for g in order], axis=0
    ).astype(BF16)

    def hop(stage, q, src, dst, to):
        return pltpu.make_async_remote_copy(
            src, dst, st_send.at[stage, q], st_recv.at[stage, q], device_id=to
        )

    def hop_a(q):
        return hop(0, q, s_a.at[q], r_a.at[q], sibling)

    def hop_bp(q):
        return hop(1, q, s_bp.at[q], r_bp.at[q], above)

    def hop_bm(q):
        return hop(2, q, s_bm.at[q], r_bm.at[q], below)

    def hop_cp(q):
        return hop(3, q, s_cp.at[q], r_cp.at[q], above)

    def hop_cm(q):
        return hop(4, q, s_cm.at[q], r_cm.at[q], below)

    def hop_d(q):
        return hop(5, q, s_d.at[q], r_d.at[q], across)

    def compute(q):
        feats = rft[q]
        inner = jnp.dot(slabn[...], feats, preferred_element_type=F32)
        gauss = jnp.exp(inner - rsq[q] - ssq[:, :1])
        w = (coup[q] * gauss).astype(BF16)
        wf = w.astype(F32)
        wide = jnp.sum(wf, axis=0, keepdims=True) * (1.0 / D)
        prod = jnp.dot(slabp[...], w, preferred_element_type=F32)
        halves = []
        for cc in range(2):
            own = jnp.concatenate(
                [
                    feats[g * 16 : g * 16 + 16].astype(F32)
                    for g in order[cc * 8 : cc * 8 + 8]
                ],
                axis=0,
            )
            halves.append(prod[cc * 128 : cc * 128 + 128] - wide * own)
        mine = core == 0
        kept[q] = jnp.where(mine, halves[0], halves[1]).reshape(4, 2, 16, RQ)
        s_a[q] = jnp.where(mine, halves[1], halves[0]).astype(BF16).reshape(4, 2, 16, RQ)
        hop_a(q).start()
        acc[...] += jnp.dot(
            w, rf[pl.ds(pl.multiple_of(q * RQ, RQ), RQ), :], preferred_element_type=F32
        )
        part = wf[:, :128]
        for lane in range(128, RQ, 128):
            part = part + wf[:, lane : lane + 128]
        wcol[...] += part

    def exchange(peer, slot):
        return pltpu.make_async_remote_copy(
            g_send.at[peer], g_recv.at[slot], g_ssem.at[peer], g_rsem.at[slot],
            device_id={"row": peer, "col": col},
        )

    def slab_side():
        total = jnp.sum(wcol[...], axis=1, keepdims=True)
        grad = acc[...] * (1.0 / D) - total * slabn[...].astype(F32)
        pieces = grad.T.reshape(N_ROW, 8, COLS)
        g_own[...] = pieces
        g_send[...] = pieces.astype(BF16)

        def send(d, c):
            exchange(lax.rem(row + d, N_ROW), row).start()
            return c

        lax.fori_loop(1, N_ROW, send, 0)
        g_recv[row] = jnp.zeros((8, COLS), BF16)

    def stage_b(q):
        hop_a(q).wait_recv()
        total = kept[q] + r_a[q].astype(F32)
        kept[q] = total
        s_bp[q] = kept[q, far, 0].astype(BF16)
        s_bm[q] = kept[q, far, 1].astype(BF16)
        hop_bp(q).start()
        hop_bm(q).start()

    def stage_c(q):
        hop_bp(q).wait_recv()
        s_cp[q, 0] = (kept[q, up, 0] + r_bp[q].astype(F32)).astype(BF16)
        s_cp[q, 1] = kept[q, up, 1].astype(BF16)
        hop_cp(q).start()
        hop_bm(q).wait_recv()
        s_cm[q, 0] = kept[q, down, 0].astype(BF16)
        s_cm[q, 1] = (kept[q, down, 1] + r_bm[q].astype(F32)).astype(BF16)
        hop_cm(q).start()

    def stage_d(q):
        hop_cp(q).wait_recv()
        hop_cm(q).wait_recv()
        there, here = 1 - hi, hi
        s_d[q] = (
            kept[q, y, there] + r_cp[q, there].astype(F32) + r_cm[q, there].astype(F32)
        ).astype(BF16)
        hop_d(q).start()
        kept[q, y, here] = (
            kept[q, y, here] + r_cp[q, here].astype(F32) + r_cm[q, here].astype(F32)
        )

    def stage_e(q):
        hop_d(q).wait_recv()
        row_out[:, pl.ds(pl.multiple_of(q * RQ, RQ), RQ)] = kept[q, y, hi] + r_d[
            q
        ].astype(F32)

    def step(t, c):
        pl.when(t < CHUNKS)(lambda: compute(t))
        pl.when(t == CHUNKS - 1)(slab_side)
        for lag, stage in zip(LAG, (stage_b, stage_c, stage_d, stage_e)):
            q = t - lag

            @pl.when((q >= 0) & (q < CHUNKS))
            def _(q=q, stage=stage):
                stage(q)

        return c

    lax.fori_loop(0, CHUNKS + LAG[-1], step, 0)

    def got_grad(d, c):
        peer = lax.rem(row + d, N_ROW)
        exchange(peer, peer).wait_recv()
        return c

    lax.fori_loop(1, N_ROW, got_grad, 0)
    slab_out[...] = g_own[row] + jnp.sum(g_recv[...].astype(F32), axis=0)

    def sent(d, c):
        peer = lax.rem(row + d, N_ROW)
        gather(peer, row).wait_send()
        exchange(peer, row).wait_send()
        return c

    lax.fori_loop(1, N_ROW, sent, 0)

    def sent_rows(q, c):
        for h in (hop_a, hop_bp, hop_bm, hop_cp, hop_cm, hop_d):
            h(q).wait_send()
        return c

    lax.fori_loop(0, CHUNKS, sent_rows, 0)


def local(row_features, row_vectors, slab_features, slab_vectors):
    vmem = pl.BlockSpec(memory_space=pltpu.VMEM)
    dma = pltpu.SemaphoreType.DMA
    small = lambda dtype: pltpu.VMEM((CHUNKS, 16, RQ), dtype)
    pair = lambda dtype: pltpu.VMEM((CHUNKS, 2, 16, RQ), dtype)
    half = lambda dtype: pltpu.VMEM((CHUNKS, 4, 2, 16, RQ), dtype)
    row_t, slab_t = pl.pallas_call(
        kernel,
        out_shape=(
            jax.ShapeDtypeStruct((16, ROWS), F32),
            jax.ShapeDtypeStruct((8, COLS), F32),
        ),
        in_specs=[vmem, vmem, vmem, pl.BlockSpec(memory_space=pl.ANY)],
        out_specs=(vmem, vmem),
        scratch_shapes=[
            pltpu.VMEM((ROWS, D), BF16),
            pltpu.VMEM((CHUNKS, D, RQ), BF16),
            pltpu.VMEM((CHUNKS, 1, RQ), F32),
            pltpu.VMEM((CHUNKS, COLS, RQ), F32),
            pltpu.VMEM((N_ROW, 8, COLS), BF16),
            pltpu.VMEM((COLS, D), BF16),
            pltpu.VMEM((D, COLS), BF16),
            pltpu.VMEM((COLS, 128), F32),
            pltpu.VMEM((COLS, D), F32),
            pltpu.VMEM((COLS, 128), F32),
            half(F32), half(BF16), half(BF16),
            small(BF16), small(BF16), small(BF16), small(BF16),
            pair(BF16), pair(BF16), pair(BF16), pair(BF16),
            small(BF16), small(BF16),
            pltpu.VMEM((N_ROW, 8, COLS), F32),
            pltpu.VMEM((N_ROW, 8, COLS), BF16),
            pltpu.VMEM((N_ROW, 8, COLS), BF16),
            dma, dma((N_ROW,)), dma((N_ROW,)), dma((N_ROW,)), dma((N_ROW,)),
            dma((6, CHUNKS)), dma((6, CHUNKS)),
        ],
        compiler_params=pltpu.CompilerParams(
            collective_id=0, has_side_effects=True, vmem_limit_bytes=40 * 1024 * 1024
        ),
        cost_estimate=pl.CostEstimate(
            flops=3 * 2 * ROWS * COLS * D, bytes_accessed=4_000_000,
            transcendentals=ROWS * COLS,
        ),
    )(slab_features.T, slab_vectors, row_vectors, row_features)
    return row_t.T, slab_t.T


def solution(mesh):
    return jax.shard_map(
        local,
        mesh=mesh,
        in_specs=(P("row", None), P(None, "row"), P("col", "row"), P(None, "col")),
        out_specs=(P("row", "col"), P("col", "row")),
        check_vma=False,
    )
```

```python
import functools

import jax
import jax.numpy as jnp
from jax import lax
from jax.experimental import pallas as pl
from jax.experimental.pallas import tpu as pltpu
from jax.sharding import PartitionSpec as P

D = 256
PROBES = 16
VECS = 17
ROWS = 3072
COLS = 192
N_ROW = 32
CHUNKS = 3
RQ = ROWS // CHUNKS
LAG = 3
Z = 16
F32, BF16 = jnp.float32, jnp.bfloat16


def kernel(
    sf_hbm, sv_hbm, rv_hbm, rf_hbm,
    row_out, slab_out,
    sf, sv, rv, rf, rft, rsq, coup, slots, slabn, slabp, ssq, weights, wcol,
    kept, s_a, r_a, s_b, r_b,
    g_own, g_near, g_from, g_send, g_recv,
    in_sem, ag_send, ag_recv, g_ssem, g_rsem, near_sem, a_send, a_recv, b_send, b_recv,
):
    row, col = lax.axis_index("row"), lax.axis_index("col")
    z, lo = lax.rem(row, Z), row // Z
    y, hi, core = col // 4, lax.rem(col // 2, 2), lax.rem(col, 2)
    me = y * 2 + hi

    sibling = {"row": row, "col": col + 1 - 2 * core}
    neighbour = {"row": (1 - lo) * Z + z, "col": col}

    def z_peer(d):
        return lax.rem(z + d, Z)

    def along_z(d):
        return {"row": lo * Z + z_peer(d), "col": col}

    def column(d):
        index = lax.rem(y + d // 2, 4) * 2 + lax.rem(hi + d % 2, 2)
        return index, {"row": row, "col": index * 2 + core}

    loads = [
        pltpu.make_async_copy(src, dst, in_sem.at[i])
        for i, (src, dst) in enumerate(
            ((sf_hbm, sf), (sv_hbm, sv), (rv_hbm, rv), (rf_hbm, rf))
        )
    ]
    for load in loads:
        load.start()

    barrier = pltpu.get_barrier_semaphore()

    def greet(d, c):
        pl.semaphore_signal(barrier, inc=1, device_id=along_z(d))
        return c

    lax.fori_loop(1, Z, greet, 0)
    for other in [sibling, neighbour] + [column(d)[1] for d in range(1, 8)]:
        pl.semaphore_signal(barrier, inc=1, device_id=other)
    loads[0].wait()
    slots[row] = sf[...]
    pl.semaphore_wait(barrier, Z - 1 + 9)

    def gather(d):
        return pltpu.make_async_remote_copy(
            sf, slots.at[row], ag_send.at[d], ag_recv.at[row], device_id=along_z(d)
        )

    def piece(slot):
        return pltpu.make_async_remote_copy(
            slots.at[slot], slots.at[slot], ag_send.at[Z + lax.rem(slot, Z)],
            ag_recv.at[slot], device_id=neighbour,
        )

    def zigzag(k):
        return jnp.where(lax.rem(k, 2) == 1, (k + 1) // 2, Z - k // 2)

    def send_slab(k, c):
        gather(zigzag(Z - k)).start()
        return c

    lax.fori_loop(1, Z, send_slab, 0)
    piece(row).start()

    first = lax.broadcasted_iota(jnp.int32, (VECS, COLS), 0) == 0
    loads[1].wait()
    scaled = (sv[...].astype(F32) * jnp.where(first, 0.5, -0.5 / PROBES)).T.astype(BF16)
    loads[2].wait()
    loads[3].wait()

    def rows(q):
        return pl.ds(pl.multiple_of(q * RQ, RQ), RQ)

    def prepare(q, c):
        wide = rf[rows(q), :].astype(F32).T
        rsq[q] = jnp.sum(wide * wide, axis=0, keepdims=True) * (0.5 / D)
        rft[q] = wide.astype(BF16)
        coup[q] = jnp.dot(scaled, rv[:, rows(q)], preferred_element_type=F32)
        return c

    lax.fori_loop(0, CHUNKS, prepare, 0)
    wcol[...] = jnp.zeros_like(wcol)

    def hand_on(k, c):
        slot = lo * Z + z_peer(zigzag(k))
        pltpu.make_async_remote_copy(
            sf, slots.at[slot], ag_send.at[0], ag_recv.at[slot], device_id=neighbour
        ).wait_recv()
        piece(slot).start()
        return c

    lax.fori_loop(1, Z, hand_on, 0)

    def got_slab(d, c):
        piece((1 - lo) * Z + z_peer(d)).wait_recv()
        return c

    lax.fori_loop(0, Z, got_slab, 0)

    slab_t = slots[...].astype(F32).reshape(D, COLS)
    slab_n = slab_t.T
    ssq[...] = jnp.broadcast_to(
        jnp.sum(slab_n * slab_n, axis=1, keepdims=True) * (0.5 / D), ssq.shape
    )
    slabn[...] = (slab_n * (1.0 / D)).astype(BF16)
    order = [b * 2 + cc for cc in range(2) for b in range(8)]
    slabp[...] = jnp.concatenate(
        [slab_t[g * 16 : g * 16 + 16] * (1.0 / D) for g in order], axis=0
    ).astype(BF16)

    def hop_a(q):
        return pltpu.make_async_remote_copy(
            s_a.at[q], r_a.at[q], a_send.at[q], a_recv.at[q], device_id=sibling
        )

    def hop_b(q, d):
        index, to = column(d)
        return pltpu.make_async_remote_copy(
            s_b.at[q, index], r_b.at[q, me], b_send.at[q, d], b_recv.at[q, me],
            device_id=to,
        )

    def compute(q):
        feats = rft[q]
        inner = jnp.dot(slabn[...], feats, preferred_element_type=F32)
        gauss = jnp.exp(inner - rsq[q] - ssq[:, :1])
        w = (coup[q] * gauss).astype(BF16)
        wf = w.astype(F32)
        wide = jnp.sum(wf, axis=0, keepdims=True) * (1.0 / D)
        prod = jnp.dot(slabp[...], w, preferred_element_type=F32)
        halves = []
        for cc in range(2):
            own = jnp.concatenate(
                [
                    feats[g * 16 : g * 16 + 16].astype(F32)
                    for g in order[cc * 8 : cc * 8 + 8]
                ],
                axis=0,
            )
            halves.append(prod[cc * 128 : cc * 128 + 128] - wide * own)
        mine = core == 0
        s_a[q] = jnp.where(mine, halves[1], halves[0]).astype(BF16).reshape(8, 16, RQ)
        hop_a(q).start()
        kept[q] = jnp.where(mine, halves[0], halves[1]).reshape(8, 16, RQ)
        weights[q] = w
        part = wf[:, :128]
        for lane in range(128, RQ, 128):
            part = part + wf[:, lane : lane + 128]
        wcol[...] += part

    def stage_b(q):
        hop_a(q).wait_recv()
        total = kept[q] + r_a[q].astype(F32)
        s_b[q] = total.astype(BF16)
        for d in (5, 4, 3, 7, 1, 2, 6):
            hop_b(q, d).start()
        kept[q, me] = kept[q, me] + r_a[q, me].astype(F32)

    def step(t, c):
        compute(t)
        pl.when(t >= LAG)(lambda: stage_b(t - LAG))
        return c

    lax.fori_loop(0, CHUNKS, step, 0)

    near = pltpu.make_async_remote_copy(
        g_near, g_from, near_sem.at[0], near_sem.at[1], device_id=neighbour
    )

    def products(q, grad):
        return grad + jnp.dot(weights[q], rf[rows(q), :], preferred_element_type=F32)

    grad = lax.fori_loop(0, CHUNKS, products, jnp.zeros((COLS, D), F32))
    total = jnp.sum(wcol[...], axis=1, keepdims=True)
    grad = grad * (1.0 / D) - total * slabn[...].astype(F32)
    g_own[...] = grad.T.reshape(2, Z, 8, COLS)
    g_near[...] = g_own[1 - lo].astype(BF16)
    near.start()
    lax.fori_loop(CHUNKS - LAG, CHUNKS, lambda q, c: (stage_b(q), c)[1], 0)
    near.wait_recv()
    g_own[lo] = g_own[lo] + g_from[...].astype(F32)
    g_send[...] = g_own[lo].astype(BF16)

    def exchange(d):
        return pltpu.make_async_remote_copy(
            g_send.at[z_peer(d)], g_recv.at[z], g_ssem.at[d], g_rsem.at[z],
            device_id=along_z(d),
        )

    def send_grad(k, c):
        exchange(zigzag(Z - k)).start()
        return c

    lax.fori_loop(1, Z, send_grad, 0)
    g_recv[z] = jnp.zeros((8, COLS), BF16)

    def finish(q, c):
        total = kept[q, me]
        for d in (1, 2, 6, 3, 7, 4, 5):
            index = column(d)[0]
            pltpu.make_async_remote_copy(
                s_b.at[q, index], r_b.at[q, index], b_send.at[q, d],
                b_recv.at[q, index], device_id=sibling,
            ).wait_recv()
            total = total + r_b[q, index].astype(F32)
        row_out[:, rows(q)] = total
        return c

    lax.fori_loop(0, CHUNKS, finish, 0)

    def got_grad(d, c):
        peer = z_peer(d)
        pltpu.make_async_remote_copy(
            g_send.at[peer], g_recv.at[peer], g_ssem.at[d], g_rsem.at[peer],
            device_id=neighbour,
        ).wait_recv()
        return c

    lax.fori_loop(1, Z, got_grad, 0)
    slab_out[...] = g_own[lo, z] + jnp.sum(g_recv[...].astype(F32), axis=0)

    near.wait_send()

    def sent(d, c):
        gather(d).wait_send()
        exchange(d).wait_send()
        return c

    lax.fori_loop(1, Z, sent, 0)

    def sent_pieces(k, c):
        piece(lo * Z + k).wait_send()
        return c

    lax.fori_loop(0, Z, sent_pieces, 0)

    def sent_rows(q, c):
        hop_a(q).wait_send()
        for d in range(1, 8):
            hop_b(q, d).wait_send()
        return c

    lax.fori_loop(0, CHUNKS, sent_rows, 0)


def local(row_features, row_vectors, slab_features, slab_vectors):
    vmem = pl.BlockSpec(memory_space=pltpu.VMEM)
    hbm = pl.BlockSpec(memory_space=pltpu.MemorySpace.HBM)
    dma = pltpu.SemaphoreType.DMA
    part = lambda dtype: pltpu.VMEM((CHUNKS, 8, 16, RQ), dtype)
    row_t, slab_t = pl.pallas_call(
        kernel,
        out_shape=(
            jax.ShapeDtypeStruct((16, ROWS), F32),
            jax.ShapeDtypeStruct((8, COLS), F32),
        ),
        in_specs=[hbm, hbm, hbm, hbm],
        out_specs=(vmem, vmem),
        scratch_shapes=[
            pltpu.VMEM((8, COLS), BF16),
            pltpu.VMEM((VECS, COLS), BF16),
            pltpu.VMEM((VECS, ROWS), BF16),
            pltpu.VMEM((ROWS, D), BF16),
            pltpu.VMEM((CHUNKS, D, RQ), BF16),
            pltpu.VMEM((CHUNKS, 1, RQ), F32),
            pltpu.VMEM((CHUNKS, COLS, RQ), F32),
            pltpu.VMEM((N_ROW, 8, COLS), BF16),
            pltpu.VMEM((COLS, D), BF16),
            pltpu.VMEM((D, COLS), BF16),
            pltpu.VMEM((COLS, 128), F32),
            pltpu.VMEM((CHUNKS, COLS, RQ), BF16),
            pltpu.VMEM((COLS, 128), F32),
            part(F32), part(BF16), part(BF16), part(BF16), part(BF16),
            pltpu.VMEM((2, Z, 8, COLS), F32),
            pltpu.VMEM((Z, 8, COLS), BF16),
            pltpu.VMEM((Z, 8, COLS), BF16),
            pltpu.VMEM((Z, 8, COLS), BF16),
            pltpu.VMEM((Z, 8, COLS), BF16),
            dma((4,)), dma((2 * Z,)), dma((N_ROW,)), dma((Z,)), dma((Z,)), dma((2,)),
            dma((CHUNKS,)), dma((CHUNKS,)), dma((CHUNKS, 8)), dma((CHUNKS, 8)),
        ],
        compiler_params=pltpu.CompilerParams(
            collective_id=0, has_side_effects=True, vmem_limit_bytes=56 * 1024 * 1024
        ),
        cost_estimate=pl.CostEstimate(
            flops=3 * 2 * ROWS * COLS * D, bytes_accessed=4_000_000,
            transcendentals=ROWS * COLS,
        ),
    )(slab_features.T, slab_vectors, row_vectors, row_features)
    return row_t.T, slab_t.T


def solution(mesh):
    return jax.shard_map(
        local,
        mesh=mesh,
        in_specs=(P("row", None), P(None, "row"), P("col", "row"), P(None, "col")),
        out_specs=(P("row", "col"), P("col", "row")),
        check_vma=False,
    )
```

```python
import functools

import jax
import jax.numpy as jnp
from jax import lax
from jax.experimental import pallas as pl
from jax.experimental.pallas import tpu as pltpu
from jax.sharding import PartitionSpec as P

D = 256
PROBES = 16
VECS = 17
ROWS = 3072
COLS = 192
N_ROW = 32
CHUNKS = 2
RQ = ROWS // CHUNKS
LAG = 2
Z = 16
F32, BF16 = jnp.float32, jnp.bfloat16


def kernel(
    sf_hbm, sv_hbm, rv_hbm, rf_hbm,
    row_out, slab_out,
    sf, sv, rv, rf, rft, rsq, coup, slots, slabn, slabp, ssq, weights, wcol,
    kept, s_a, r_a, s_b, r_b, row_v, slab_v,
    g_own, g_near, g_from, g_send, g_recv,
    in_sem, ag_send, ag_recv, g_ssem, g_rsem, near_sem, a_send, a_recv, b_send, b_recv, out_sem,
):
    row, col = lax.axis_index("row"), lax.axis_index("col")
    z, lo = lax.rem(row, Z), row // Z
    y, hi, core = col // 4, lax.rem(col // 2, 2), lax.rem(col, 2)
    me = y * 2 + hi

    sibling = {"row": row, "col": col + 1 - 2 * core}
    neighbour = {"row": (1 - lo) * Z + z, "col": col}

    def z_peer(d):
        return lax.rem(z + d, Z)

    def along_z(d):
        return {"row": lo * Z + z_peer(d), "col": col}

    def column(d):
        index = lax.rem(y + d // 2, 4) * 2 + lax.rem(hi + d % 2, 2)
        return index, {"row": row, "col": index * 2 + core}

    loads = [
        pltpu.make_async_copy(src, dst, in_sem.at[i])
        for i, (src, dst) in enumerate(
            ((sf_hbm, sf), (sv_hbm, sv), (rv_hbm, rv), (rf_hbm, rf))
        )
    ]
    for load in loads:
        load.start()

    barrier = pltpu.get_barrier_semaphore()

    def greet(d, c):
        pl.semaphore_signal(barrier, inc=1, device_id=along_z(d))
        return c

    lax.fori_loop(1, Z, greet, 0)
    for other in [sibling, neighbour] + [column(d)[1] for d in range(1, 8)]:
        pl.semaphore_signal(barrier, inc=1, device_id=other)
    loads[0].wait()
    slots[row] = sf[...]
    pl.semaphore_wait(barrier, Z - 1 + 9)

    def gather(d):
        return pltpu.make_async_remote_copy(
            sf, slots.at[row], ag_send.at[d], ag_recv.at[row], device_id=along_z(d)
        )

    def piece(slot):
        return pltpu.make_async_remote_copy(
            slots.at[slot], slots.at[slot], ag_send.at[Z + lax.rem(slot, Z)],
            ag_recv.at[slot], device_id=neighbour,
        )

    def zigzag(k):
        return jnp.where(lax.rem(k, 2) == 1, (k + 1) // 2, Z - k // 2)

    def send_slab(k, c):
        gather(zigzag(Z - k)).start()
        return c

    lax.fori_loop(1, Z, send_slab, 0)
    piece(row).start()

    first = lax.broadcasted_iota(jnp.int32, (VECS, COLS), 0) == 0
    loads[1].wait()
    scaled = (sv[...].astype(F32) * jnp.where(first, 0.5, -0.5 / PROBES)).T.astype(BF16)
    loads[2].wait()
    loads[3].wait()

    def rows(q):
        return pl.ds(pl.multiple_of(q * RQ, RQ), RQ)

    def prepare(q, c):
        wide = rf[rows(q), :].astype(F32).T
        rsq[q] = jnp.sum(wide * wide, axis=0, keepdims=True) * (0.5 / D)
        rft[q] = wide.astype(BF16)
        coup[q] = jnp.dot(scaled, rv[:, rows(q)], preferred_element_type=F32)
        return c

    lax.fori_loop(0, CHUNKS, prepare, 0)
    wcol[...] = jnp.zeros_like(wcol)

    def hand_on(k, c):
        slot = lo * Z + z_peer(zigzag(k))
        pltpu.make_async_remote_copy(
            sf, slots.at[slot], ag_send.at[0], ag_recv.at[slot], device_id=neighbour
        ).wait_recv()
        piece(slot).start()
        return c

    lax.fori_loop(1, Z, hand_on, 0)

    def got_slab(d, c):
        piece((1 - lo) * Z + z_peer(d)).wait_recv()
        return c

    lax.fori_loop(0, Z, got_slab, 0)

    slab_t = slots[...].astype(F32).reshape(D, COLS)
    slab_n = slab_t.T
    ssq[...] = jnp.broadcast_to(
        jnp.sum(slab_n * slab_n, axis=1, keepdims=True) * (0.5 / D), ssq.shape
    )
    slabn[...] = (slab_n * (1.0 / D)).astype(BF16)
    order = [b * 2 + cc for cc in range(2) for b in range(8)]
    slabp[...] = jnp.concatenate(
        [slab_t[g * 16 : g * 16 + 16] * (1.0 / D) for g in order], axis=0
    ).astype(BF16)

    def hop_a(q):
        return pltpu.make_async_remote_copy(
            s_a.at[q], r_a.at[q], a_send.at[q], a_recv.at[q], device_id=sibling
        )

    def hop_b(q, d):
        index, to = column(d)
        return pltpu.make_async_remote_copy(
            s_b.at[q, index], r_b.at[q, me], b_send.at[q, d], b_recv.at[q, me],
            device_id=to,
        )

    def compute(q):
        feats = rft[q]
        inner = jnp.dot(slabn[...], feats, preferred_element_type=F32)
        gauss = jnp.exp(inner - rsq[q] - ssq[:, :1])
        w = (coup[q] * gauss).astype(BF16)
        wf = w.astype(F32)
        wide = jnp.sum(wf, axis=0, keepdims=True) * (1.0 / D)
        prod = jnp.dot(slabp[...], w, preferred_element_type=F32)
        halves = []
        for cc in range(2):
            own = jnp.concatenate(
                [
                    feats[g * 16 : g * 16 + 16].astype(F32)
                    for g in order[cc * 8 : cc * 8 + 8]
                ],
                axis=0,
            )
            halves.append(prod[cc * 128 : cc * 128 + 128] - wide * own)
        mine = core == 0
        s_a[q] = jnp.where(mine, halves[1], halves[0]).astype(BF16).reshape(8, 16, RQ)
        hop_a(q).start()
        kept[q] = jnp.where(mine, halves[0], halves[1]).reshape(8, 16, RQ)
        weights[q] = w
        part = wf[:, :128]
        for lane in range(128, RQ, 128):
            part = part + wf[:, lane : lane + 128]
        wcol[...] += part

    def stage_b(q):
        hop_a(q).wait_recv()
        total = kept[q] + r_a[q].astype(F32)
        s_b[q] = total.astype(BF16)
        for d in (5, 4, 3, 7, 1, 2, 6):
            hop_b(q, d).start()
        kept[q, me] = kept[q, me] + r_a[q, me].astype(F32)

    def step(t, c):
        compute(t)
        pl.when(t >= LAG)(lambda: stage_b(t - LAG))
        return c

    lax.fori_loop(0, CHUNKS, step, 0)

    near = pltpu.make_async_remote_copy(
        g_near, g_from, near_sem.at[0], near_sem.at[1], device_id=neighbour
    )

    def products(q, grad):
        return grad + jnp.dot(weights[q], rf[rows(q), :], preferred_element_type=F32)

    grad = lax.fori_loop(0, CHUNKS, products, jnp.zeros((COLS, D), F32))
    total = jnp.sum(wcol[...], axis=1, keepdims=True)
    grad = grad * (1.0 / D) - total * slabn[...].astype(F32)
    g_own[...] = grad.T.reshape(2, Z, 8, COLS)
    g_near[...] = g_own[1 - lo].astype(BF16)
    near.start()
    lax.fori_loop(CHUNKS - LAG, CHUNKS, lambda q, c: (stage_b(q), c)[1], 0)
    near.wait_recv()
    g_own[lo] = g_own[lo] + g_from[...].astype(F32)
    g_send[...] = g_own[lo].astype(BF16)

    def exchange(d):
        return pltpu.make_async_remote_copy(
            g_send.at[z_peer(d)], g_recv.at[z], g_ssem.at[d], g_rsem.at[z],
            device_id=along_z(d),
        )

    def send_grad(k, c):
        exchange(zigzag(Z - k)).start()
        return c

    lax.fori_loop(1, Z, send_grad, 0)
    g_recv[z] = jnp.zeros((8, COLS), BF16)

    def result(q):
        return pltpu.make_async_copy(
            row_v.at[:, rows(q)], row_out.at[:, rows(q)], out_sem.at[q]
        )

    def finish(q, c):
        total = kept[q, me]
        for d in (1, 2, 6, 3, 7, 4, 5):
            index = column(d)[0]
            pltpu.make_async_remote_copy(
                s_b.at[q, index], r_b.at[q, index], b_send.at[q, d],
                b_recv.at[q, index], device_id=sibling,
            ).wait_recv()
            total = total + r_b[q, index].astype(F32)
        row_v[:, rows(q)] = total
        result(q).start()
        return c

    lax.fori_loop(0, CHUNKS, finish, 0)

    def got_grad(d, c):
        peer = z_peer(d)
        pltpu.make_async_remote_copy(
            g_send.at[peer], g_recv.at[peer], g_ssem.at[d], g_rsem.at[peer],
            device_id=neighbour,
        ).wait_recv()
        return c

    lax.fori_loop(1, Z, got_grad, 0)
    slab_v[...] = g_own[lo, z] + jnp.sum(g_recv[...].astype(F32), axis=0)
    slab_result = pltpu.make_async_copy(slab_v, slab_out, out_sem.at[CHUNKS])
    slab_result.start()
    for q in range(CHUNKS):
        result(q).wait()
    slab_result.wait()

    near.wait_send()

    def sent(d, c):
        gather(d).wait_send()
        exchange(d).wait_send()
        return c

    lax.fori_loop(1, Z, sent, 0)

    def sent_pieces(k, c):
        piece(lo * Z + k).wait_send()
        return c

    lax.fori_loop(0, Z, sent_pieces, 0)

    def sent_rows(q, c):
        hop_a(q).wait_send()
        for d in range(1, 8):
            hop_b(q, d).wait_send()
        return c

    lax.fori_loop(0, CHUNKS, sent_rows, 0)


def place(row_in, slab_in, row_out, slab_out):
    row_out[...] = row_in[...]
    slab_out[...] = slab_in[...]


def local(row_features, row_vectors, slab_features, slab_vectors):
    vmem = pl.BlockSpec(memory_space=pltpu.VMEM)
    hbm = pl.BlockSpec(memory_space=pltpu.MemorySpace.HBM)
    dma = pltpu.SemaphoreType.DMA
    part = lambda dtype: pltpu.VMEM((CHUNKS, 8, 16, RQ), dtype)
    row_t, slab_t = pl.pallas_call(
        kernel,
        out_shape=(
            jax.ShapeDtypeStruct((16, ROWS), F32),
            jax.ShapeDtypeStruct((8, COLS), F32),
        ),
        in_specs=[hbm, hbm, hbm, hbm],
        out_specs=(hbm, hbm),
        scratch_shapes=[
            pltpu.VMEM((8, COLS), BF16),
            pltpu.VMEM((VECS, COLS), BF16),
            pltpu.VMEM((VECS, ROWS), BF16),
            pltpu.VMEM((ROWS, D), BF16),
            pltpu.VMEM((CHUNKS, D, RQ), BF16),
            pltpu.VMEM((CHUNKS, 1, RQ), F32),
            pltpu.VMEM((CHUNKS, COLS, RQ), F32),
            pltpu.VMEM((N_ROW, 8, COLS), BF16),
            pltpu.VMEM((COLS, D), BF16),
            pltpu.VMEM((D, COLS), BF16),
            pltpu.VMEM((COLS, 128), F32),
            pltpu.VMEM((CHUNKS, COLS, RQ), BF16),
            pltpu.VMEM((COLS, 128), F32),
            part(F32), part(BF16), part(BF16), part(BF16), part(BF16),
            pltpu.VMEM((16, ROWS), F32), pltpu.VMEM((8, COLS), F32),
            pltpu.VMEM((2, Z, 8, COLS), F32),
            pltpu.VMEM((Z, 8, COLS), BF16),
            pltpu.VMEM((Z, 8, COLS), BF16),
            pltpu.VMEM((Z, 8, COLS), BF16),
            pltpu.VMEM((Z, 8, COLS), BF16),
            dma((4,)), dma((2 * Z,)), dma((N_ROW,)), dma((Z,)), dma((Z,)), dma((2,)),
            dma((CHUNKS,)), dma((CHUNKS,)), dma((CHUNKS, 8)), dma((CHUNKS, 8)), dma((CHUNKS + 1,)),
        ],
        compiler_params=pltpu.CompilerParams(
            collective_id=0, has_side_effects=True, vmem_limit_bytes=56 * 1024 * 1024
        ),
        cost_estimate=pl.CostEstimate(
            flops=3 * 2 * ROWS * COLS * D, bytes_accessed=4_000_000,
            transcendentals=ROWS * COLS,
        ),
    )(slab_features.T, slab_vectors, row_vectors, row_features)
    row_t, slab_t = pl.pallas_call(
        place,
        out_shape=(
            jax.ShapeDtypeStruct((16, ROWS), F32),
            jax.ShapeDtypeStruct((8, COLS), F32),
        ),
        in_specs=[vmem, vmem],
        out_specs=(vmem, vmem),
        compiler_params=pltpu.CompilerParams(vmem_limit_bytes=56 * 1024 * 1024),
    )(row_t, slab_t)
    return row_t.T, slab_t.T


def solution(mesh):
    return jax.shard_map(
        local,
        mesh=mesh,
        in_specs=(P("row", None), P(None, "row"), P("col", "row"), P(None, "col")),
        out_specs=(P("row", "col"), P("col", "row")),
        check_vma=False,
    )
```

```python
import functools

import jax
import jax.numpy as jnp
from jax import lax
from jax.experimental import pallas as pl
from jax.experimental.pallas import tpu as pltpu
from jax.sharding import PartitionSpec as P

D = 256
PROBES = 16
VECS = 17
ROWS = 3072
COLS = 192
N_ROW = 32
CHUNKS = 2
RQ = ROWS // CHUNKS
LAG = 2
NEAR = 7
Z = 16
F32, BF16 = jnp.float32, jnp.bfloat16


def kernel(
    sf_hbm, sv_hbm, rv_hbm, rf_hbm,
    row_out, slab_out,
    sf, sv, rv, rf, rft, rsq, coup, slots, slabn, slabp, ssq, weights, wcol,
    kept, s_a, r_a, s_b, r_b, row_v, slab_v,
    g_own, g_near, g_from, g_send, g_recv,
    in_sem, ag_send, ag_recv, g_ssem, g_rsem, near_sem, a_send, a_recv, b_send, b_recv, out_sem,
):
    row, col = lax.axis_index("row"), lax.axis_index("col")
    z, lo = lax.rem(row, Z), row // Z
    y, hi, core = col // 4, lax.rem(col // 2, 2), lax.rem(col, 2)
    me = y * 2 + hi

    sibling = {"row": row, "col": col + 1 - 2 * core}
    neighbour = {"row": (1 - lo) * Z + z, "col": col}

    def z_peer(d):
        return lax.rem(z + d, Z)

    def along_z(d):
        return {"row": lo * Z + z_peer(d), "col": col}

    def beside_z(d):
        return {"row": (1 - lo) * Z + z_peer(d), "col": col}

    def column(d):
        index = lax.rem(y + d // 2, 4) * 2 + lax.rem(hi + d % 2, 2)
        return index, {"row": row, "col": index * 2 + core}

    loads = [
        pltpu.make_async_copy(src, dst, in_sem.at[i])
        for i, (src, dst) in enumerate(
            ((sf_hbm, sf), (sv_hbm, sv), (rv_hbm, rv), (rf_hbm, rf))
        )
    ]
    for load in loads:
        load.start()

    barrier = pltpu.get_barrier_semaphore()

    def zigzag(k):
        return jnp.where(lax.rem(k, 2) == 1, (k + 1) // 2, Z - k // 2)

    def greet(k, c):
        pl.semaphore_signal(barrier, inc=1, device_id=along_z(zigzag(Z - k)))
        return c

    def greet_far(k, c):
        pl.semaphore_signal(barrier, inc=1, device_id=beside_z(zigzag(Z - k)))
        return c

    FAR = Z - 1 - 2 * NEAR
    lax.fori_loop(1, FAR + 1, greet_far, 0)
    lax.fori_loop(1, Z, greet, 0)
    for other in [column(d)[1] for d in (5, 4, 3, 7, 1, 2, 6)] + [neighbour, sibling]:
        pl.semaphore_signal(barrier, inc=1, device_id=other)
    loads[0].wait()
    slots[row] = sf[...]
    pl.semaphore_wait(barrier, Z - 1 + FAR + 9)

    def gather(d):
        return pltpu.make_async_remote_copy(
            sf, slots.at[row], ag_send.at[d], ag_recv.at[row], device_id=along_z(d)
        )

    def piece(slot):
        return pltpu.make_async_remote_copy(
            slots.at[slot], slots.at[slot], ag_send.at[Z + lax.rem(slot, Z)],
            ag_recv.at[slot], device_id=neighbour,
        )

    def gather_far(d):
        return pltpu.make_async_remote_copy(
            sf, slots.at[row], ag_send.at[2 * Z + d], ag_recv.at[row],
            device_id=beside_z(d),
        )

    def send_far(k, c):
        gather_far(zigzag(Z - k)).start()
        gather(zigzag(Z - k)).start()
        return c

    def send_near(k, c):
        gather(zigzag(Z - k)).start()
        return c

    lax.fori_loop(1, FAR + 1, send_far, 0)
    lax.fori_loop(FAR + 1, Z, send_near, 0)
    piece(row).start()

    first = lax.broadcasted_iota(jnp.int32, (VECS, COLS), 0) == 0
    loads[1].wait()
    scaled = (sv[...].astype(F32) * jnp.where(first, 0.5, -0.5 / PROBES)).T.astype(BF16)
    loads[2].wait()
    loads[3].wait()

    def rows(q):
        return pl.ds(pl.multiple_of(q * RQ, RQ), RQ)

    def prepare(q, c):
        wide = rf[rows(q), :].astype(F32).T
        rsq[q] = jnp.sum(wide * wide, axis=0, keepdims=True) * (0.5 / D)
        rft[q] = wide.astype(BF16)
        coup[q] = jnp.dot(scaled, rv[:, rows(q)], preferred_element_type=F32)
        return c

    lax.fori_loop(0, CHUNKS, prepare, 0)
    wcol[...] = jnp.zeros_like(wcol)

    def hand_on(k, c):
        slot = lo * Z + z_peer(zigzag(k))
        pltpu.make_async_remote_copy(
            sf, slots.at[slot], ag_send.at[0], ag_recv.at[slot], device_id=neighbour
        ).wait_recv()
        piece(slot).start()
        return c

    lax.fori_loop(1, 2 * NEAR + 1, hand_on, 0)

    def arrived(slot):
        pltpu.make_async_remote_copy(
            sf, slots.at[slot], ag_send.at[0], ag_recv.at[slot], device_id=neighbour
        ).wait_recv()

    def got_far(k, c):
        arrived(lo * Z + z_peer(zigzag(k)))
        return c

    def got_beside(d, c):
        arrived((1 - lo) * Z + z_peer(d))
        return c

    lax.fori_loop(2 * NEAR + 1, Z, got_far, 0)
    lax.fori_loop(0, Z, got_beside, 0)

    slab_t = slots[...].astype(F32).reshape(D, COLS)
    slab_n = slab_t.T
    ssq[...] = jnp.broadcast_to(
        jnp.sum(slab_n * slab_n, axis=1, keepdims=True) * (0.5 / D), ssq.shape
    )
    slabn[...] = (slab_n * (1.0 / D)).astype(BF16)
    for half in range(2):
        at = pl.multiple_of(lax.rem(half + core, 2) * (D // 2), D // 2)
        slabp[pl.ds(at, D // 2)] = jnp.concatenate(
            [slab_t[b * 32 + half * 16 : b * 32 + half * 16 + 16] * (1.0 / D) for b in range(8)],
            axis=0,
        ).astype(BF16)

    def half_of(q, which):
        return jnp.concatenate(
            [
                rft[q, pl.ds(pl.multiple_of(b * 32 + which * 16, 16), 16)].astype(F32)
                for b in range(8)
            ],
            axis=0,
        )

    def hop_a(q):
        return pltpu.make_async_remote_copy(
            s_a.at[q], r_a.at[q], a_send.at[q], a_recv.at[q], device_id=sibling
        )

    def hop_b(q, d):
        index, to = column(d)
        return pltpu.make_async_remote_copy(
            s_b.at[q, index], r_b.at[q, me], b_send.at[q, d], b_recv.at[q, me],
            device_id=to,
        )

    def compute(q):
        feats = rft[q]
        inner = jnp.dot(slabn[...], feats, preferred_element_type=F32)
        gauss = jnp.exp(inner - rsq[q] - ssq[:, :1])
        w = (coup[q] * gauss).astype(BF16)
        wf = w.astype(F32)
        wide = jnp.sum(wf, axis=0, keepdims=True) * (1.0 / D)
        prod = jnp.dot(slabp[...], w, preferred_element_type=F32)
        theirs = prod[D // 2 :] - wide * half_of(q, 1 - core)
        s_a[q] = theirs.astype(BF16).reshape(8, 16, RQ)
        hop_a(q).start()
        kept[q] = (prod[: D // 2] - wide * half_of(q, core)).reshape(8, 16, RQ)
        weights[q] = w
        part = wf[:, :128]
        for lane in range(128, RQ, 128):
            part = part + wf[:, lane : lane + 128]
        wcol[...] += part

    def stage_b(q):
        hop_a(q).wait_recv()
        total = kept[q] + r_a[q].astype(F32)
        s_b[q] = total.astype(BF16)
        for d in (5, 4, 3, 7, 1, 2, 6):
            hop_b(q, d).start()
        kept[q, me] = kept[q, me] + r_a[q, me].astype(F32)

    def step(t, c):
        compute(t)
        pl.when(t >= LAG)(lambda: stage_b(t - LAG))
        return c

    lax.fori_loop(0, CHUNKS, step, 0)

    near = pltpu.make_async_remote_copy(
        g_near, g_from, near_sem.at[0], near_sem.at[1], device_id=neighbour
    )

    def products(q, grad):
        return grad + jnp.dot(weights[q], rf[rows(q), :], preferred_element_type=F32)

    grad = lax.fori_loop(0, CHUNKS, products, jnp.zeros((COLS, D), F32))
    total = jnp.sum(wcol[...], axis=1, keepdims=True)
    grad = grad * (1.0 / D) - total * slabn[...].astype(F32)
    g_own[...] = grad.T.reshape(2, Z, 8, COLS)
    g_near[...] = g_own[1 - lo].astype(BF16)
    near.start()
    lax.fori_loop(0, 1, lambda q, c: (stage_b(q), c)[1], 0)
    near.wait_recv()
    g_own[lo] = g_own[lo] + g_from[...].astype(F32)
    g_send[...] = g_own[lo].astype(BF16)

    def exchange(d):
        return pltpu.make_async_remote_copy(
            g_send.at[z_peer(d)], g_recv.at[z], g_ssem.at[d], g_rsem.at[z],
            device_id=along_z(d),
        )

    def send_grad(k, c):
        exchange(zigzag(Z - k)).start()
        return c

    lax.fori_loop(1, Z, send_grad, 0)
    lax.fori_loop(1, CHUNKS, lambda q, c: (stage_b(q), c)[1], 0)
    g_recv[z] = jnp.zeros((8, COLS), BF16)

    near.wait_send()

    def sent(d, c):
        gather(d).wait_send()
        return c

    lax.fori_loop(1, Z, sent, 0)

    def sent_far(k, c):
        gather_far(zigzag(Z - k)).wait_send()
        return c

    lax.fori_loop(1, FAR + 1, sent_far, 0)

    def sent_pieces(k, c):
        piece(lo * Z + z_peer(zigzag(k))).wait_send()
        return c

    lax.fori_loop(1, 2 * NEAR + 1, sent_pieces, 0)
    piece(row).wait_send()

    def sent_rows(q, c):
        hop_a(q).wait_send()
        for d in range(1, 8):
            hop_b(q, d).wait_send()
        return c

    def sent_grad(d, c):
        exchange(d).wait_send()
        return c

    def result(q):
        return pltpu.make_async_copy(
            row_v.at[:, rows(q)], row_out.at[:, rows(q)], out_sem.at[q]
        )

    def finish(q, c):
        total = kept[q, me]
        for d in (1, 2, 6, 3, 7, 4, 5):
            index = column(d)[0]
            pltpu.make_async_remote_copy(
                s_b.at[q, index], r_b.at[q, index], b_send.at[q, d],
                b_recv.at[q, index], device_id=sibling,
            ).wait_recv()
            total = total + r_b[q, index].astype(F32)
        row_v[:, rows(q)] = total
        result(q).start()
        return c

    lax.fori_loop(0, CHUNKS - 1, finish, 0)
    lax.fori_loop(0, CHUNKS, sent_rows, 0)
    lax.fori_loop(1, Z, sent_grad, 0)
    finish(CHUNKS - 1, 0)

    def got_grad(d, c):
        peer = z_peer(d)
        pltpu.make_async_remote_copy(
            g_send.at[peer], g_recv.at[peer], g_ssem.at[d], g_rsem.at[peer],
            device_id=neighbour,
        ).wait_recv()
        return c

    lax.fori_loop(1, Z, got_grad, 0)
    slab_v[...] = g_own[lo, z] + jnp.sum(g_recv[...].astype(F32), axis=0)
    slab_result = pltpu.make_async_copy(slab_v, slab_out, out_sem.at[CHUNKS])
    slab_result.start()
    for q in range(CHUNKS):
        result(q).wait()
    slab_result.wait()


def place(row_in, slab_in, row_out, slab_out):
    row_out[...] = row_in[...]
    slab_out[...] = slab_in[...]


def local(row_features, row_vectors, slab_features, slab_vectors):
    vmem = pl.BlockSpec(memory_space=pltpu.VMEM)
    hbm = pl.BlockSpec(memory_space=pltpu.MemorySpace.HBM)
    dma = pltpu.SemaphoreType.DMA
    part = lambda dtype: pltpu.VMEM((CHUNKS, 8, 16, RQ), dtype)
    row_t, slab_t = pl.pallas_call(
        kernel,
        out_shape=(
            jax.ShapeDtypeStruct((16, ROWS), F32),
            jax.ShapeDtypeStruct((8, COLS), F32),
        ),
        in_specs=[hbm, hbm, hbm, hbm],
        out_specs=(hbm, hbm),
        scratch_shapes=[
            pltpu.VMEM((8, COLS), BF16),
            pltpu.VMEM((VECS, COLS), BF16),
            pltpu.VMEM((VECS, ROWS), BF16),
            pltpu.VMEM((ROWS, D), BF16),
            pltpu.VMEM((CHUNKS, D, RQ), BF16),
            pltpu.VMEM((CHUNKS, 1, RQ), F32),
            pltpu.VMEM((CHUNKS, COLS, RQ), F32),
            pltpu.VMEM((N_ROW, 8, COLS), BF16),
            pltpu.VMEM((COLS, D), BF16),
            pltpu.VMEM((D, COLS), BF16),
            pltpu.VMEM((COLS, 128), F32),
            pltpu.VMEM((CHUNKS, COLS, RQ), BF16),
            pltpu.VMEM((COLS, 128), F32),
            part(F32), part(BF16), part(BF16), part(BF16), part(BF16),
            pltpu.VMEM((16, ROWS), F32), pltpu.VMEM((8, COLS), F32),
            pltpu.VMEM((2, Z, 8, COLS), F32),
            pltpu.VMEM((Z, 8, COLS), BF16),
            pltpu.VMEM((Z, 8, COLS), BF16),
            pltpu.VMEM((Z, 8, COLS), BF16),
            pltpu.VMEM((Z, 8, COLS), BF16),
            dma((4,)), dma((3 * Z,)), dma((N_ROW,)), dma((Z,)), dma((Z,)), dma((2,)),
            dma((CHUNKS,)), dma((CHUNKS,)), dma((CHUNKS, 8)), dma((CHUNKS, 8)), dma((CHUNKS + 1,)),
        ],
        compiler_params=pltpu.CompilerParams(
            collective_id=0, has_side_effects=True, vmem_limit_bytes=56 * 1024 * 1024
        ),
        cost_estimate=pl.CostEstimate(
            flops=3 * 2 * ROWS * COLS * D, bytes_accessed=4_000_000,
            transcendentals=ROWS * COLS,
        ),
    )(slab_features.T, slab_vectors, row_vectors, row_features)
    row_t, slab_t = pl.pallas_call(
        place,
        out_shape=(
            jax.ShapeDtypeStruct((16, ROWS), F32),
            jax.ShapeDtypeStruct((8, COLS), F32),
        ),
        in_specs=[vmem, vmem],
        out_specs=(vmem, vmem),
        compiler_params=pltpu.CompilerParams(vmem_limit_bytes=56 * 1024 * 1024),
    )(row_t, slab_t)
    return row_t.T, slab_t.T


def solution(mesh):
    return jax.shard_map(
        local,
        mesh=mesh,
        in_specs=(P("row", None), P(None, "row"), P("col", "row"), P(None, "col")),
        out_specs=(P("row", "col"), P("col", "row")),
        check_vma=False,
    )
```

```python
import functools

import jax
import jax.numpy as jnp
from jax import lax
from jax.experimental import pallas as pl
from jax.experimental.pallas import tpu as pltpu
from jax.sharding import PartitionSpec as P

D = 256
PROBES = 16
VECS = 17
ROWS = 3072
COLS = 192
N_ROW = 32
CHUNKS = 2
RQ = ROWS // CHUNKS
LAG = 2
Z = 16
F32, BF16 = jnp.float32, jnp.bfloat16


def kernel(
    sf_hbm, sv_hbm, rv_hbm, rf_hbm,
    row_out, slab_out,
    sf, sv, rv, rf, rft, rsq, coup, slots, slabn, slabp, ssq, weights, wcol,
    kept, s_a, r_a, s_b, r_b, row_v, slab_v,
    g_own, g_near, g_from, g_send, g_recv,
    in_sem, ag_send, ag_recv, g_ssem, g_rsem, near_sem, a_send, a_recv, b_send, b_recv, out_sem,
):
    row, col = lax.axis_index("row"), lax.axis_index("col")
    z, lo = lax.rem(row, Z), row // Z
    y, hi, core = col // 4, lax.rem(col // 2, 2), lax.rem(col, 2)
    me = y * 2 + hi

    sibling = {"row": row, "col": col + 1 - 2 * core}
    neighbour = {"row": (1 - lo) * Z + z, "col": col}

    def z_peer(d):
        return lax.rem(z + d, Z)

    def along_z(d):
        return {"row": lo * Z + z_peer(d), "col": col}

    def column(d):
        index = lax.rem(y + d // 2, 4) * 2 + lax.rem(hi + d % 2, 2)
        return index, {"row": row, "col": index * 2 + core}

    loads = [
        pltpu.make_async_copy(src, dst, in_sem.at[i])
        for i, (src, dst) in enumerate(
            ((sf_hbm, sf), (sv_hbm, sv), (rv_hbm, rv), (rf_hbm, rf))
        )
    ]
    for load in loads:
        load.start()

    barrier = pltpu.get_barrier_semaphore()

    def greet(d, c):
        pl.semaphore_signal(barrier, inc=1, device_id=along_z(d))
        return c

    lax.fori_loop(1, Z, greet, 0)
    for other in [sibling, neighbour] + [column(d)[1] for d in range(1, 8)]:
        pl.semaphore_signal(barrier, inc=1, device_id=other)
    loads[0].wait()
    slots[row] = sf[...]
    pl.semaphore_wait(barrier, Z - 1 + 9)

    def gather(d):
        return pltpu.make_async_remote_copy(
            sf, slots.at[row], ag_send.at[d], ag_recv.at[row], device_id=along_z(d)
        )

    def piece(slot):
        return pltpu.make_async_remote_copy(
            slots.at[slot], slots.at[slot], ag_send.at[Z + lax.rem(slot, Z)],
            ag_recv.at[slot], device_id=neighbour,
        )

    def zigzag(k):
        return jnp.where(lax.rem(k, 2) == 1, (k + 1) // 2, Z - k // 2)

    def send_slab(k, c):
        gather(zigzag(Z - k)).start()
        return c

    lax.fori_loop(1, Z, send_slab, 0)
    piece(row).start()

    first = lax.broadcasted_iota(jnp.int32, (VECS, COLS), 0) == 0
    loads[1].wait()
    scaled = (sv[...].astype(F32) * jnp.where(first, 0.5, -0.5 / PROBES)).T.astype(BF16)
    loads[2].wait()
    loads[3].wait()

    def rows(q):
        return pl.ds(pl.multiple_of(q * RQ, RQ), RQ)

    def prepare(q, c):
        wide = rf[rows(q), :].astype(F32).T
        rsq[q] = jnp.sum(wide * wide, axis=0, keepdims=True) * (0.5 / D)
        rft[q] = wide.astype(BF16)
        coup[q] = jnp.dot(scaled, rv[:, rows(q)], preferred_element_type=F32)
        return c

    lax.fori_loop(0, CHUNKS, prepare, 0)
    wcol[...] = jnp.zeros_like(wcol)

    def hand_on(k, c):
        slot = lo * Z + z_peer(zigzag(k))
        pltpu.make_async_remote_copy(
            sf, slots.at[slot], ag_send.at[0], ag_recv.at[slot], device_id=neighbour
        ).wait_recv()
        piece(slot).start()
        return c

    lax.fori_loop(1, Z, hand_on, 0)

    def got_slab(d, c):
        piece((1 - lo) * Z + z_peer(d)).wait_recv()
        return c

    lax.fori_loop(0, Z, got_slab, 0)

    slab_t = slots[...].astype(F32).reshape(D, COLS)
    slab_n = slab_t.T
    ssq[...] = jnp.broadcast_to(
        jnp.sum(slab_n * slab_n, axis=1, keepdims=True) * (0.5 / D), ssq.shape
    )
    slabn[...] = (slab_n * (1.0 / D)).astype(BF16)
    for half in range(2):
        at = pl.multiple_of(lax.rem(half + core, 2) * (D // 2), D // 2)
        slabp[pl.ds(at, D // 2)] = jnp.concatenate(
            [slab_t[b * 32 + half * 16 : b * 32 + half * 16 + 16] * (1.0 / D) for b in range(8)],
            axis=0,
        ).astype(BF16)

    def half_of(q, which):
        return jnp.concatenate(
            [
                rft[q, pl.ds(pl.multiple_of(b * 32 + which * 16, 16), 16)].astype(F32)
                for b in range(8)
            ],
            axis=0,
        )

    def hop_a(q):
        return pltpu.make_async_remote_copy(
            s_a.at[q], r_a.at[q], a_send.at[q], a_recv.at[q], device_id=sibling
        )

    def hop_b(q, d):
        index, to = column(d)
        return pltpu.make_async_remote_copy(
            s_b.at[q, index], r_b.at[q, me], b_send.at[q, d], b_recv.at[q, me],
            device_id=to,
        )

    def compute(q):
        feats = rft[q]
        inner = jnp.dot(slabn[...], feats, preferred_element_type=F32)
        gauss = jnp.exp(inner - rsq[q] - ssq[:, :1])
        w = (coup[q] * gauss).astype(BF16)
        wf = w.astype(F32)
        wide = jnp.sum(wf, axis=0, keepdims=True) * (1.0 / D)
        prod = jnp.dot(slabp[...], w, preferred_element_type=F32)
        theirs = prod[D // 2 :] - wide * half_of(q, 1 - core)
        s_a[q] = theirs.astype(BF16).reshape(8, 16, RQ)
        hop_a(q).start()
        kept[q] = (prod[: D // 2] - wide * half_of(q, core)).reshape(8, 16, RQ)
        weights[q] = w
        part = wf[:, :128]
        for lane in range(128, RQ, 128):
            part = part + wf[:, lane : lane + 128]
        wcol[...] += part

    def stage_b(q):
        hop_a(q).wait_recv()
        total = kept[q] + r_a[q].astype(F32)
        s_b[q] = total.astype(BF16)
        for d in (5, 4, 3, 7, 1, 2, 6):
            hop_b(q, d).start()
        kept[q, me] = kept[q, me] + r_a[q, me].astype(F32)

    def step(t, c):
        compute(t)
        pl.when(t >= LAG)(lambda: stage_b(t - LAG))
        return c

    lax.fori_loop(0, CHUNKS, step, 0)

    near = pltpu.make_async_remote_copy(
        g_near, g_from, near_sem.at[0], near_sem.at[1], device_id=neighbour
    )

    def products(q, grad):
        return grad + jnp.dot(weights[q], rf[rows(q), :], preferred_element_type=F32)

    grad = lax.fori_loop(0, CHUNKS, products, jnp.zeros((COLS, D), F32))
    total = jnp.sum(wcol[...], axis=1, keepdims=True)
    grad = grad * (1.0 / D) - total * slabn[...].astype(F32)
    g_own[...] = grad.T.reshape(2, Z, 8, COLS)
    g_near[...] = g_own[1 - lo].astype(BF16)
    near.start()
    lax.fori_loop(CHUNKS - LAG, CHUNKS, lambda q, c: (stage_b(q), c)[1], 0)
    near.wait_recv()
    g_own[lo] = g_own[lo] + g_from[...].astype(F32)
    g_send[...] = g_own[lo].astype(BF16)

    def exchange(d):
        return pltpu.make_async_remote_copy(
            g_send.at[z_peer(d)], g_recv.at[z], g_ssem.at[d], g_rsem.at[z],
            device_id=along_z(d),
        )

    def send_grad(k, c):
        exchange(zigzag(Z - k)).start()
        return c

    lax.fori_loop(1, Z, send_grad, 0)
    g_recv[z] = jnp.zeros((8, COLS), BF16)

    def result(q):
        return pltpu.make_async_copy(
            row_v.at[:, rows(q)], row_out.at[:, rows(q)], out_sem.at[q]
        )

    def finish(q, c):
        total = kept[q, me]
        for d in (1, 2, 6, 3, 7, 4, 5):
            index = column(d)[0]
            pltpu.make_async_remote_copy(
                s_b.at[q, index], r_b.at[q, index], b_send.at[q, d],
                b_recv.at[q, index], device_id=sibling,
            ).wait_recv()
            total = total + r_b[q, index].astype(F32)
        row_v[:, rows(q)] = total
        result(q).start()
        return c

    lax.fori_loop(0, CHUNKS, finish, 0)

    def got_grad(d, c):
        peer = z_peer(d)
        pltpu.make_async_remote_copy(
            g_send.at[peer], g_recv.at[peer], g_ssem.at[d], g_rsem.at[peer],
            device_id=neighbour,
        ).wait_recv()
        return c

    lax.fori_loop(1, Z, got_grad, 0)
    slab_v[...] = g_own[lo, z] + jnp.sum(g_recv[...].astype(F32), axis=0)
    slab_result = pltpu.make_async_copy(slab_v, slab_out, out_sem.at[CHUNKS])
    slab_result.start()
    for q in range(CHUNKS):
        result(q).wait()
    slab_result.wait()

    near.wait_send()

    def sent(d, c):
        gather(d).wait_send()
        exchange(d).wait_send()
        return c

    lax.fori_loop(1, Z, sent, 0)

    def sent_pieces(k, c):
        piece(lo * Z + k).wait_send()
        return c

    lax.fori_loop(0, Z, sent_pieces, 0)

    def sent_rows(q, c):
        hop_a(q).wait_send()
        for d in range(1, 8):
            hop_b(q, d).wait_send()
        return c

    lax.fori_loop(0, CHUNKS, sent_rows, 0)


def place(row_in, slab_in, row_out, slab_out):
    row_out[...] = row_in[...]
    slab_out[...] = slab_in[...]


def local(row_features, row_vectors, slab_features, slab_vectors):
    vmem = pl.BlockSpec(memory_space=pltpu.VMEM)
    hbm = pl.BlockSpec(memory_space=pltpu.MemorySpace.HBM)
    dma = pltpu.SemaphoreType.DMA
    part = lambda dtype: pltpu.VMEM((CHUNKS, 8, 16, RQ), dtype)
    row_t, slab_t = pl.pallas_call(
        kernel,
        out_shape=(
            jax.ShapeDtypeStruct((16, ROWS), F32),
            jax.ShapeDtypeStruct((8, COLS), F32),
        ),
        in_specs=[hbm, hbm, hbm, hbm],
        out_specs=(hbm, hbm),
        scratch_shapes=[
            pltpu.VMEM((8, COLS), BF16),
            pltpu.VMEM((VECS, COLS), BF16),
            pltpu.VMEM((VECS, ROWS), BF16),
            pltpu.VMEM((ROWS, D), BF16),
            pltpu.VMEM((CHUNKS, D, RQ), BF16),
            pltpu.VMEM((CHUNKS, 1, RQ), F32),
            pltpu.VMEM((CHUNKS, COLS, RQ), F32),
            pltpu.VMEM((N_ROW, 8, COLS), BF16),
            pltpu.VMEM((COLS, D), BF16),
            pltpu.VMEM((D, COLS), BF16),
            pltpu.VMEM((COLS, 128), F32),
            pltpu.VMEM((CHUNKS, COLS, RQ), BF16),
            pltpu.VMEM((COLS, 128), F32),
            part(F32), part(BF16), part(BF16), part(BF16), part(BF16),
            pltpu.VMEM((16, ROWS), F32), pltpu.VMEM((8, COLS), F32),
            pltpu.VMEM((2, Z, 8, COLS), F32),
            pltpu.VMEM((Z, 8, COLS), BF16),
            pltpu.VMEM((Z, 8, COLS), BF16),
            pltpu.VMEM((Z, 8, COLS), BF16),
            pltpu.VMEM((Z, 8, COLS), BF16),
            dma((4,)), dma((2 * Z,)), dma((N_ROW,)), dma((Z,)), dma((Z,)), dma((2,)),
            dma((CHUNKS,)), dma((CHUNKS,)), dma((CHUNKS, 8)), dma((CHUNKS, 8)), dma((CHUNKS + 1,)),
        ],
        compiler_params=pltpu.CompilerParams(
            collective_id=0, has_side_effects=True, vmem_limit_bytes=56 * 1024 * 1024
        ),
        cost_estimate=pl.CostEstimate(
            flops=3 * 2 * ROWS * COLS * D, bytes_accessed=4_000_000,
            transcendentals=ROWS * COLS,
        ),
    )(slab_features.T, slab_vectors, row_vectors, row_features)
    row_t, slab_t = pl.pallas_call(
        place,
        out_shape=(
            jax.ShapeDtypeStruct((16, ROWS), F32),
            jax.ShapeDtypeStruct((8, COLS), F32),
        ),
        in_specs=[vmem, vmem],
        out_specs=(vmem, vmem),
        compiler_params=pltpu.CompilerParams(vmem_limit_bytes=56 * 1024 * 1024),
    )(row_t, slab_t)
    return row_t.T, slab_t.T


def solution(mesh):
    return jax.shard_map(
        local,
        mesh=mesh,
        in_specs=(P("row", None), P(None, "row"), P("col", "row"), P(None, "col")),
        out_specs=(P("row", "col"), P("col", "row")),
        check_vma=False,
    )
```

```python
import functools

import jax
import jax.numpy as jnp
from jax import lax
from jax.experimental import pallas as pl
from jax.experimental.pallas import tpu as pltpu
from jax.sharding import PartitionSpec as P

D = 256
PROBES = 16
VECS = 17
ROWS = 3072
COLS = 192
N_ROW = 32
CHUNKS = 2
RQ = ROWS // CHUNKS
LAG = 2
Z = 16
F32, BF16 = jnp.float32, jnp.bfloat16


def kernel(
    sf_hbm, sv_hbm, rv_hbm, rf_hbm,
    row_out, slab_out,
    sf, sv, rv, rf, rft, rsq, coup, slots, slabn, slabp, ssq, weights, wcol,
    kept, s_a, r_a, s_b, r_b, row_v, slab_v,
    g_own, g_near, g_from, g_send, g_recv,
    in_sem, ag_send, ag_recv, g_ssem, g_rsem, near_sem, a_send, a_recv, b_send, b_recv, out_sem,
):
    row, col = lax.axis_index("row"), lax.axis_index("col")
    z, lo = lax.rem(row, Z), row // Z
    y, hi, core = col // 4, lax.rem(col // 2, 2), lax.rem(col, 2)
    me = y * 2 + hi

    sibling = {"row": row, "col": col + 1 - 2 * core}
    neighbour = {"row": (1 - lo) * Z + z, "col": col}

    def z_peer(d):
        return lax.rem(z + d, Z)

    def along_z(d):
        return {"row": lo * Z + z_peer(d), "col": col}

    def column(d):
        index = lax.rem(y + d // 2, 4) * 2 + lax.rem(hi + d % 2, 2)
        return index, {"row": row, "col": index * 2 + core}

    loads = [
        pltpu.make_async_copy(src, dst, in_sem.at[i])
        for i, (src, dst) in enumerate(
            ((sf_hbm, sf), (sv_hbm, sv), (rv_hbm, rv), (rf_hbm, rf))
        )
    ]
    for load in loads:
        load.start()

    barrier = pltpu.get_barrier_semaphore()

    def zigzag(k):
        return jnp.where(lax.rem(k, 2) == 1, (k + 1) // 2, Z - k // 2)

    def greet(k, c):
        pl.semaphore_signal(barrier, inc=1, device_id=along_z(zigzag(Z - k)))
        return c

    lax.fori_loop(1, Z, greet, 0)
    for other in [sibling, neighbour] + [column(d)[1] for d in range(1, 8)]:
        pl.semaphore_signal(barrier, inc=1, device_id=other)
    loads[0].wait()
    slots[row] = sf[...]
    pl.semaphore_wait(barrier, Z - 1 + 9)

    def gather(d):
        return pltpu.make_async_remote_copy(
            sf, slots.at[row], ag_send.at[d], ag_recv.at[row], device_id=along_z(d)
        )

    def piece(slot):
        return pltpu.make_async_remote_copy(
            slots.at[slot], slots.at[slot], ag_send.at[Z + lax.rem(slot, Z)],
            ag_recv.at[slot], device_id=neighbour,
        )

    def send_slab(k, c):
        gather(zigzag(Z - k)).start()
        return c

    lax.fori_loop(1, Z, send_slab, 0)
    piece(row).start()

    first = lax.broadcasted_iota(jnp.int32, (VECS, COLS), 0) == 0
    loads[1].wait()
    scaled = (sv[...].astype(F32) * jnp.where(first, 0.5, -0.5 / PROBES)).T.astype(BF16)
    loads[2].wait()
    loads[3].wait()

    def rows(q):
        return pl.ds(pl.multiple_of(q * RQ, RQ), RQ)

    def prepare(q, c):
        wide = rf[rows(q), :].astype(F32).T
        rsq[q] = jnp.sum(wide * wide, axis=0, keepdims=True) * (0.5 / D)
        rft[q] = wide.astype(BF16)
        coup[q] = jnp.dot(scaled, rv[:, rows(q)], preferred_element_type=F32)
        return c

    lax.fori_loop(0, CHUNKS, prepare, 0)
    wcol[...] = jnp.zeros_like(wcol)

    def hand_on(k, c):
        slot = lo * Z + z_peer(zigzag(k))
        pltpu.make_async_remote_copy(
            sf, slots.at[slot], ag_send.at[0], ag_recv.at[slot], device_id=neighbour
        ).wait_recv()
        piece(slot).start()
        return c

    lax.fori_loop(1, Z, hand_on, 0)

    def got_slab(d, c):
        piece((1 - lo) * Z + z_peer(d)).wait_recv()
        return c

    lax.fori_loop(0, Z, got_slab, 0)

    slab_t = slots[...].astype(F32).reshape(D, COLS)
    slab_n = slab_t.T
    ssq[...] = jnp.broadcast_to(
        jnp.sum(slab_n * slab_n, axis=1, keepdims=True) * (0.5 / D), ssq.shape
    )
    slabn[...] = (slab_n * (1.0 / D)).astype(BF16)
    for half in range(2):
        at = pl.multiple_of(lax.rem(half + core, 2) * (D // 2), D // 2)
        slabp[pl.ds(at, D // 2)] = jnp.concatenate(
            [slab_t[b * 32 + half * 16 : b * 32 + half * 16 + 16] * (1.0 / D) for b in range(8)],
            axis=0,
        ).astype(BF16)

    def half_of(q, which):
        return jnp.concatenate(
            [
                rft[q, pl.ds(pl.multiple_of(b * 32 + which * 16, 16), 16)].astype(F32)
                for b in range(8)
            ],
            axis=0,
        )

    def hop_a(q):
        return pltpu.make_async_remote_copy(
            s_a.at[q], r_a.at[q], a_send.at[q], a_recv.at[q], device_id=sibling
        )

    def hop_b(q, d):
        index, to = column(d)
        return pltpu.make_async_remote_copy(
            s_b.at[q, index], r_b.at[q, me], b_send.at[q, d], b_recv.at[q, me],
            device_id=to,
        )

    def compute(q):
        feats = rft[q]
        inner = jnp.dot(slabn[...], feats, preferred_element_type=F32)
        gauss = jnp.exp(inner - rsq[q] - ssq[:, :1])
        w = (coup[q] * gauss).astype(BF16)
        wf = w.astype(F32)
        wide = jnp.sum(wf, axis=0, keepdims=True) * (1.0 / D)
        prod = jnp.dot(slabp[...], w, preferred_element_type=F32)
        theirs = prod[D // 2 :] - wide * half_of(q, 1 - core)
        s_a[q] = theirs.astype(BF16).reshape(8, 16, RQ)
        hop_a(q).start()
        kept[q] = (prod[: D // 2] - wide * half_of(q, core)).reshape(8, 16, RQ)
        weights[q] = w
        part = wf[:, :128]
        for lane in range(128, RQ, 128):
            part = part + wf[:, lane : lane + 128]
        wcol[...] += part

    def stage_b(q):
        hop_a(q).wait_recv()
        total = kept[q] + r_a[q].astype(F32)
        s_b[q] = total.astype(BF16)
        for d in (5, 4, 3, 7, 1, 2, 6):
            hop_b(q, d).start()
        kept[q, me] = kept[q, me] + r_a[q, me].astype(F32)

    def step(t, c):
        compute(t)
        pl.when(t >= LAG)(lambda: stage_b(t - LAG))
        return c

    lax.fori_loop(0, CHUNKS, step, 0)

    near = pltpu.make_async_remote_copy(
        g_near, g_from, near_sem.at[0], near_sem.at[1], device_id=neighbour
    )

    def products(q, grad):
        return grad + jnp.dot(weights[q], rf[rows(q), :], preferred_element_type=F32)

    grad = lax.fori_loop(0, CHUNKS, products, jnp.zeros((COLS, D), F32))
    total = jnp.sum(wcol[...], axis=1, keepdims=True)
    grad = grad * (1.0 / D) - total * slabn[...].astype(F32)
    g_own[...] = grad.T.reshape(2, Z, 8, COLS)
    g_near[...] = g_own[1 - lo].astype(BF16)
    near.start()
    lax.fori_loop(CHUNKS - LAG, CHUNKS, lambda q, c: (stage_b(q), c)[1], 0)
    near.wait_recv()
    g_own[lo] = g_own[lo] + g_from[...].astype(F32)
    g_send[...] = g_own[lo].astype(BF16)

    def exchange(d):
        return pltpu.make_async_remote_copy(
            g_send.at[z_peer(d)], g_recv.at[z], g_ssem.at[d], g_rsem.at[z],
            device_id=along_z(d),
        )

    def send_grad(k, c):
        exchange(zigzag(Z - k)).start()
        return c

    lax.fori_loop(1, Z, send_grad, 0)
    g_recv[z] = jnp.zeros((8, COLS), BF16)

    def result(q):
        return pltpu.make_async_copy(
            row_v.at[:, rows(q)], row_out.at[:, rows(q)], out_sem.at[q]
        )

    def finish(q, c):
        total = kept[q, me]
        for d in (1, 2, 6, 3, 7, 4, 5):
            index = column(d)[0]
            pltpu.make_async_remote_copy(
                s_b.at[q, index], r_b.at[q, index], b_send.at[q, d],
                b_recv.at[q, index], device_id=sibling,
            ).wait_recv()
            total = total + r_b[q, index].astype(F32)
        row_v[:, rows(q)] = total
        result(q).start()
        return c

    lax.fori_loop(0, CHUNKS, finish, 0)

    def got_grad(d, c):
        peer = z_peer(d)
        pltpu.make_async_remote_copy(
            g_send.at[peer], g_recv.at[peer], g_ssem.at[d], g_rsem.at[peer],
            device_id=neighbour,
        ).wait_recv()
        return c

    lax.fori_loop(1, Z, got_grad, 0)
    slab_v[...] = g_own[lo, z] + jnp.sum(g_recv[...].astype(F32), axis=0)
    slab_result = pltpu.make_async_copy(slab_v, slab_out, out_sem.at[CHUNKS])
    slab_result.start()
    for q in range(CHUNKS):
        result(q).wait()
    slab_result.wait()

    near.wait_send()

    def sent(d, c):
        gather(d).wait_send()
        exchange(d).wait_send()
        return c

    lax.fori_loop(1, Z, sent, 0)

    def sent_pieces(k, c):
        piece(lo * Z + k).wait_send()
        return c

    lax.fori_loop(0, Z, sent_pieces, 0)

    def sent_rows(q, c):
        hop_a(q).wait_send()
        for d in range(1, 8):
            hop_b(q, d).wait_send()
        return c

    lax.fori_loop(0, CHUNKS, sent_rows, 0)


def place(row_in, slab_in, row_out, slab_out):
    row_out[...] = row_in[...]
    slab_out[...] = slab_in[...]


def local(row_features, row_vectors, slab_features, slab_vectors):
    vmem = pl.BlockSpec(memory_space=pltpu.VMEM)
    hbm = pl.BlockSpec(memory_space=pltpu.MemorySpace.HBM)
    dma = pltpu.SemaphoreType.DMA
    part = lambda dtype: pltpu.VMEM((CHUNKS, 8, 16, RQ), dtype)
    row_t, slab_t = pl.pallas_call(
        kernel,
        out_shape=(
            jax.ShapeDtypeStruct((16, ROWS), F32),
            jax.ShapeDtypeStruct((8, COLS), F32),
        ),
        in_specs=[hbm, hbm, hbm, hbm],
        out_specs=(hbm, hbm),
        scratch_shapes=[
            pltpu.VMEM((8, COLS), BF16),
            pltpu.VMEM((VECS, COLS), BF16),
            pltpu.VMEM((VECS, ROWS), BF16),
            pltpu.VMEM((ROWS, D), BF16),
            pltpu.VMEM((CHUNKS, D, RQ), BF16),
            pltpu.VMEM((CHUNKS, 1, RQ), F32),
            pltpu.VMEM((CHUNKS, COLS, RQ), F32),
            pltpu.VMEM((N_ROW, 8, COLS), BF16),
            pltpu.VMEM((COLS, D), BF16),
            pltpu.VMEM((D, COLS), BF16),
            pltpu.VMEM((COLS, 128), F32),
            pltpu.VMEM((CHUNKS, COLS, RQ), BF16),
            pltpu.VMEM((COLS, 128), F32),
            part(F32), part(BF16), part(BF16), part(BF16), part(BF16),
            pltpu.VMEM((16, ROWS), F32), pltpu.VMEM((8, COLS), F32),
            pltpu.VMEM((2, Z, 8, COLS), F32),
            pltpu.VMEM((Z, 8, COLS), BF16),
            pltpu.VMEM((Z, 8, COLS), BF16),
            pltpu.VMEM((Z, 8, COLS), BF16),
            pltpu.VMEM((Z, 8, COLS), BF16),
            dma((4,)), dma((2 * Z,)), dma((N_ROW,)), dma((Z,)), dma((Z,)), dma((2,)),
            dma((CHUNKS,)), dma((CHUNKS,)), dma((CHUNKS, 8)), dma((CHUNKS, 8)), dma((CHUNKS + 1,)),
        ],
        compiler_params=pltpu.CompilerParams(
            collective_id=0, has_side_effects=True, vmem_limit_bytes=56 * 1024 * 1024
        ),
        cost_estimate=pl.CostEstimate(
            flops=3 * 2 * ROWS * COLS * D, bytes_accessed=4_000_000,
            transcendentals=ROWS * COLS,
        ),
    )(slab_features.T, slab_vectors, row_vectors, row_features)
    row_t, slab_t = pl.pallas_call(
        place,
        out_shape=(
            jax.ShapeDtypeStruct((16, ROWS), F32),
            jax.ShapeDtypeStruct((8, COLS), F32),
        ),
        in_specs=[vmem, vmem],
        out_specs=(vmem, vmem),
        compiler_params=pltpu.CompilerParams(vmem_limit_bytes=56 * 1024 * 1024),
    )(row_t, slab_t)
    return row_t.T, slab_t.T


def solution(mesh):
    return jax.shard_map(
        local,
        mesh=mesh,
        in_specs=(P("row", None), P(None, "row"), P("col", "row"), P(None, "col")),
        out_specs=(P("row", "col"), P("col", "row")),
        check_vma=False,
    )
```
